32 devices in a mesh: grp: 2 (over x), ka: 16 (over z, y, core).
Axes of the slice: x: 2, y: 2, z: 4, core: 2. Of those that a mesh axis runs over, the one named last changes fastest.
Arguments:
- coefficients: bfloat16 [2, 512, 32768], P(None, 'ka'), may hold values from -768 to 768
- occ_weight: float32 [16, 32], replicated, may hold values from 0.02 to 1
- virt_weight: float32 [16, 32], replicated, may hold values from 0.02 to 1
- partner: int32 [32], P('grp'), parts along dimension 0, may hold values from 0 to 15, as said below
- points: int32 [1536], replicated, may hold values from 0 to 32767, as said below
Outputs:
- polarizability: float32 [4, 16, 384, 384], P('grp', 'ka'), parts along dimension 0
The draws below stay inside these ranges and needn't reach their ends.
There are 2 independent parts, one for each index of `grp`. The reference program is written for one: setup_inputs(seed, part) draws one part's arguments, and reference() takes and returns one part's arrays. A program takes and returns all parts, laid end to end along the dimension named above; an argument that names none is the same for every part. Nothing has to cross between parts.
Inputs may be any that keep to these rules, and one draw needn't show every extreme that they name: 1536 distinct grid points. Every k-point is the partner of exactly one k-point.
All inputs are finite; a program needn't handle non-finite values.
Results may differ from the reference program's by a relative error of at most 0.0016.
Values may be sent and summed in bfloat16 or wider, within the bound.
A program may use at most 192 MiB of HBM per device.

```python
import math
from functools import partial
import jax
import jax.numpy as jnp
from jax import lax

NG = 32
GRID = 32768
NMU = 1536
KPTS = 16
BANDS = 32
STATES = 512
COLB = 4
ROWB = 4
BROW = 384
BCOL = 384


def draw_coefficients(key, part):
    array_shape = (2, STATES, GRID)
    rough_part = jnp.clip(jax.random.normal(key, array_shape, jnp.float32), -6.0, 6.0)
    lift_factor = 4.0 * NG
    zero_mode = jnp.arange(GRID) == 0
    return jnp.where(zero_mode[None, None, :], rough_part * lift_factor, rough_part).astype(jnp.bfloat16)


def draw_points(key, part):
    first_key, second_key = jax.random.split(key)
    interior = 1 + jax.random.permutation(first_key, GRID - 2)[:NMU - 2]
    extremes = jnp.array([0, GRID - 1], dtype=jnp.int32)
    chosen = jnp.concatenate([extremes, interior.astype(jnp.int32)])
    return jax.random.permutation(second_key, chosen).astype(jnp.int32)


def draw_partner(key, part):
    own_key = jax.random.fold_in(key, 7)
    return jax.random.permutation(own_key, KPTS).astype(jnp.int32)


def setup_inputs(seed: int = 0, part: int = 0) -> dict:
    arg_keys = jax.random.split(jax.random.key(seed), 6)
    part_splits = jax.random.split(jax.random.fold_in(arg_keys[5], part), 6)
    coefficients = draw_coefficients(jax.random.fold_in(arg_keys[5], 71), part)
    occ_weight = jnp.clip(jnp.exp(jax.random.uniform(arg_keys[1], (KPTS, BANDS), jnp.float32, math.log(0.02), math.log(1.0))), 0.02, 1.0)
    virt_weight = jnp.clip(jnp.exp(jax.random.uniform(arg_keys[2], (KPTS, BANDS), jnp.float32, math.log(0.02), math.log(1.0))), 0.02, 1.0)
    partner = draw_partner(jax.random.fold_in(jax.random.fold_in(arg_keys[5], part), 71), part)
    points = draw_points(jax.random.fold_in(arg_keys[5], 71), part)
    return dict(coefficients=coefficients, occ_weight=occ_weight, virt_weight=virt_weight, partner=partner, points=points)


def orbital_values(state_block, points):
    coef_field = state_block[0].astype(jnp.float32) + 1j * state_block[1].astype(jnp.float32)
    coef_field = coef_field.reshape(BANDS, NG, NG, NG)
    wave_values = jnp.fft.ifftn(coef_field, axes=(1, 2, 3), norm="ortho").reshape(BANDS, NG ** 3)
    wave_values = jnp.take(wave_values, points, axis=1)
    return jnp.stack([jnp.real(wave_values), jnp.imag(wave_values)]).astype(jnp.bfloat16)


def density(orbitals, weight):
    scaled = (orbitals.astype(jnp.float32) * weight[None, :, None]).astype(jnp.bfloat16)
    right_side = jnp.concatenate([orbitals[0], orbitals[1]], axis=0)
    left_real = jnp.concatenate([scaled[0], scaled[1]], axis=0)
    left_imag = jnp.concatenate([scaled[1], -scaled[0]], axis=0)
    real_part = jnp.dot(left_real.T, right_side, preferred_element_type=jnp.float32)
    imag_part = jnp.dot(left_imag.T, right_side, preferred_element_type=jnp.float32)
    return real_part, imag_part


def reference(coefficients, occ_weight, virt_weight, partner, points):
    blocks = coefficients.reshape(2, KPTS, BANDS, NG ** 3).transpose(1, 0, 2, 3)
    orbitals = lax.map(partial(orbital_values, points=points), blocks)
    real_sum = jnp.zeros((NMU, NMU), jnp.float32)
    imag_sum = jnp.zeros((NMU, NMU), jnp.float32)
    for kpoint in range(KPTS):
        occ_real, occ_imag = density(orbitals[kpoint], occ_weight[kpoint])
        partner_index = partner[kpoint]
        virt_real, virt_imag = density(orbitals[partner_index], virt_weight[partner_index])
        real_sum = real_sum + occ_real * virt_real + occ_imag * virt_imag
        imag_sum = imag_sum + occ_imag * virt_real - occ_real * virt_imag
    scaling = 1.0 / (BANDS * BANDS)
    full_value = jnp.stack([real_sum, imag_sum]) * scaling
    blocked = full_value.reshape(2, ROWB, BROW, COLB, BCOL).transpose(0, 1, 3, 2, 4)
    return blocked.reshape(2, ROWB * COLB, BROW, BCOL)
```

```python
import functools
import math

import jax
import jax.numpy as jnp
from jax import lax
from jax.experimental import pallas as pl
from jax.experimental.pallas import tpu as pltpu
from jax.sharding import PartitionSpec as P

NG = 32
PLANE = NG * NG
GROUP = 8
VMEM_LIMIT = 56 * 1024 * 1024


def phase_rows(frequency, targets):
    angles = ((frequency * targets) % NG).astype(jnp.float32) * (2.0 * math.pi / NG)
    return jnp.cos(angles), jnp.sin(angles)


def orbital_kernel(chunk, pts_ref, coef_ref, out_ref, lhs, cos_hi, sin_hi, cos_lo, sin_lo, xcos, xsin, acc):
    step = pl.program_id(0)
    states = coef_ref.shape[1]
    count = pts_ref.shape[1]

    @pl.when(step == 0)
    def _():
        pts = pts_ref[...]
        frequency = lax.broadcasted_iota(jnp.int32, (NG, count), 0)
        norm = 1.0 / math.sqrt(NG**3)
        cos_x, sin_x = phase_rows(frequency, pts // PLANE)
        xcos[...] = cos_x * norm
        xsin[...] = sin_x * norm
        cos_y, sin_y = phase_rows(frequency, pts // NG % NG)
        cos_z, sin_z = phase_rows(frequency, pts % NG)
        for gy in range(NG):
            rows = slice(gy * NG, (gy + 1) * NG)
            cy, sy = cos_y[gy : gy + 1], sin_y[gy : gy + 1]
            cos_t = cy * cos_z - sy * sin_z
            sin_t = sy * cos_z + cy * sin_z
            high = cos_t.astype(jnp.bfloat16)
            cos_hi[rows] = high
            cos_lo[rows] = (cos_t - high.astype(jnp.float32)).astype(jnp.bfloat16)
            high = sin_t.astype(jnp.bfloat16)
            sin_hi[rows] = high
            sin_lo[rows] = (sin_t - high.astype(jnp.float32)).astype(jnp.bfloat16)
        acc[...] = jnp.zeros_like(acc)

    for j in range(GROUP):
        for c in range(2):
            start = (2 * j + c) * states
            lhs[start : start + states] = coef_ref[c, :, j * PLANE : (j + 1) * PLANE]

    def dot(table, low, cols):
        left = lhs[...]
        return jnp.dot(left, table[:, cols], preferred_element_type=jnp.float32) + jnp.dot(
            left, low[:, cols], preferred_element_type=jnp.float32
        )

    gx = pl.ds(pl.multiple_of(step * GROUP, GROUP), GROUP)
    for m in range(count // chunk):
        cols = slice(m * chunk, (m + 1) * chunk)
        by_cos = dot(cos_hi, cos_lo, cols)
        by_sin = dot(sin_hi, sin_lo, cols)
        pc, ps = xcos[gx, cols], xsin[gx, cols]
        real_sum, imag_sum = acc[0, :, cols], acc[1, :, cols]
        for j in range(GROUP):
            a = slice(2 * j * states, (2 * j + 1) * states)
            b = slice((2 * j + 1) * states, (2 * j + 2) * states)
            re = by_cos[a] - by_sin[b]
            im = by_sin[a] + by_cos[b]
            c, s = pc[j : j + 1], ps[j : j + 1]
            real_sum = real_sum + (re * c - im * s)
            imag_sum = imag_sum + (re * s + im * c)
        acc[0, :, cols] = real_sum
        acc[1, :, cols] = imag_sum

    @pl.when(step == pl.num_programs(0) - 1)
    def _():
        out_ref[...] = acc[...].astype(jnp.bfloat16)


def orbitals_at(coefficients, points):
    states = coefficients.shape[1]
    count = points.shape[0]
    chunk = 256 if count % 256 == 0 else 128
    table = pltpu.VMEM((PLANE, count), jnp.bfloat16)
    return pl.pallas_call(
        functools.partial(orbital_kernel, chunk),
        grid=(NG // GROUP,),
        out_shape=jax.ShapeDtypeStruct((2, states, count), jnp.bfloat16),
        in_specs=[
            pl.BlockSpec((1, count), lambda i: (0, 0)),
            pl.BlockSpec((2, states, GROUP * PLANE), lambda i: (0, 0, i)),
        ],
        out_specs=pl.BlockSpec((2, states, count), lambda i: (0, 0, 0)),
        scratch_shapes=[
            pltpu.VMEM((GROUP * 2 * states, PLANE), jnp.bfloat16),
            table, table, table, table,
            pltpu.VMEM((NG, count), jnp.float32),
            pltpu.VMEM((NG, count), jnp.float32),
            pltpu.VMEM((2, states, count), jnp.float32),
        ],
        compiler_params=pltpu.CompilerParams(vmem_limit_bytes=VMEM_LIMIT),
        name="orbitals",
    )(points.reshape(1, count), coefficients)


def polar_kernel(partner_ref, row_ref, col_ref, occ_ref, virt_ref, out_ref):
    kpoints, parts, bands, _ = row_ref.shape
    scaling = 1.0 / (bands * bands)
    dims = (((0,), (0,)), ((), ()))

    def density(k, weight_ref):
        rows = row_ref[k].astype(jnp.float32)
        weighted = (rows * weight_ref[k][None]).astype(jnp.bfloat16)
        cols = col_ref[k]
        right = jnp.concatenate([cols[0], cols[1]], axis=0)
        real_left = jnp.concatenate([weighted[0], weighted[1]], axis=0)
        imag_left = jnp.concatenate([weighted[1], -weighted[0]], axis=0)
        return (
            lax.dot_general(real_left, right, dims, preferred_element_type=jnp.float32),
            lax.dot_general(imag_left, right, dims, preferred_element_type=jnp.float32),
        )

    def step(k, carry):
        occ_real, occ_imag = density(k, occ_ref)
        virt_real, virt_imag = density(partner_ref[k], virt_ref)
        out_ref[0, 0] += (occ_real * virt_real + occ_imag * virt_imag) * scaling
        out_ref[1, 0] += (occ_imag * virt_real - occ_real * virt_imag) * scaling
        return carry

    out_ref[...] = jnp.zeros_like(out_ref)
    lax.fori_loop(0, kpoints, step, 0)


def polarizability(partner, row_side, col_side, occ_weight, virt_weight):
    row_len, col_len = row_side.shape[3], col_side.shape[3]
    vmem = pl.BlockSpec(memory_space=pltpu.VMEM)
    return pl.pallas_call(
        polar_kernel,
        out_shape=jax.ShapeDtypeStruct((2, 1, row_len, col_len), jnp.float32),
        in_specs=[pl.BlockSpec(memory_space=pltpu.SMEM), vmem, vmem, vmem, vmem],
        out_specs=vmem,
        compiler_params=pltpu.CompilerParams(vmem_limit_bytes=VMEM_LIMIT),
        name="polarizability",
    )(partner, row_side, col_side, occ_weight[:, :, None], virt_weight[:, :, None])


def body(coefficients, occ_weight, virt_weight, partner, points):
    devices = lax.axis_size("ka")
    groups = lax.axis_size("grp")
    col_blocks = min(16, max(4, devices // 8))
    row_blocks = devices // col_blocks
    kpoints, bands = occ_weight.shape
    point_count = points.shape[0]
    states = coefficients.shape[1]
    row_len = point_count // row_blocks
    col_len = point_count // col_blocks
    share = point_count // groups
    mine = lax.dynamic_slice_in_dim(points, lax.axis_index("grp") * share, share)
    orbitals = orbitals_at(coefficients, mine)
    orbitals = lax.all_gather(orbitals, "grp", axis=2, tiled=True)
    planes = [list(range(r * col_blocks, (r + 1) * col_blocks)) for r in range(row_blocks)]
    lines = [list(range(c, devices, col_blocks)) for c in range(col_blocks)]

    def split(count):
        return jnp.transpose(orbitals.reshape(2, states, count, -1), (2, 0, 1, 3))

    rows = split(row_blocks)
    rows = lax.all_to_all(rows, "ka", 0, 0, axis_index_groups=lines, tiled=True)
    rows = lax.all_gather(rows, "ka", axis=0, axis_index_groups=planes)
    rows = jnp.swapaxes(rows, 0, 1)
    cols = split(col_blocks)
    cols = lax.all_to_all(cols, "ka", 0, 0, axis_index_groups=planes, tiled=True)
    cols = lax.all_gather(cols, "ka", axis=0, axis_index_groups=lines)

    def by_kpoint(side, length):
        side = side.reshape(kpoints, devices // kpoints, 2, states, length)
        return jnp.swapaxes(side, 1, 2).reshape(kpoints, 2, bands, length)

    return polarizability(
        partner, by_kpoint(rows, row_len), by_kpoint(cols, col_len), occ_weight, virt_weight
    )


def solution(mesh):
    return jax.shard_map(
        body,
        mesh=mesh,
        in_specs=(P(None, "ka", None), P(), P(), P("grp"), P()),
        out_specs=P("grp", "ka", None, None),
        check_vma=False,
    )
```

```python
import functools
import math

import jax
import jax.numpy as jnp
from jax import lax
from jax.experimental import pallas as pl
from jax.experimental.pallas import tpu as pltpu
from jax.sharding import PartitionSpec as P

NG = 32
PLANE = NG * NG
GROUP = 8
VMEM_LIMIT = 56 * 1024 * 1024


def phase_rows(frequency, targets):
    angles = ((frequency * targets) % NG).astype(jnp.float32) * (2.0 * math.pi / NG)
    return jnp.cos(angles), jnp.sin(angles)


def orbital_kernel(chunk, pts_ref, coef_ref, out_ref, lhs, cos_hi, sin_hi, cos_lo, sin_lo, xcos, xsin, acc):
    step = pl.program_id(0)
    states = coef_ref.shape[1]
    count = acc.shape[2]

    @pl.when(step == 0)
    def _():
        start = pl.multiple_of(lax.axis_index("grp") * count, 128)
        pts = pts_ref[:, pl.ds(start, count)]
        frequency = lax.broadcasted_iota(jnp.int32, (NG, count), 0)
        norm = 1.0 / math.sqrt(NG**3)
        cos_x, sin_x = phase_rows(frequency, pts // PLANE)
        xcos[...] = cos_x * norm
        xsin[...] = sin_x * norm
        cos_y, sin_y = phase_rows(frequency, pts // NG % NG)
        cos_z, sin_z = phase_rows(frequency, pts % NG)
        for gy in range(NG):
            rows = slice(gy * NG, (gy + 1) * NG)
            cy, sy = cos_y[gy : gy + 1], sin_y[gy : gy + 1]
            cos_t = cy * cos_z - sy * sin_z
            sin_t = sy * cos_z + cy * sin_z
            high = cos_t.astype(jnp.bfloat16)
            cos_hi[rows] = high
            cos_lo[rows] = (cos_t - high.astype(jnp.float32)).astype(jnp.bfloat16)
            high = sin_t.astype(jnp.bfloat16)
            sin_hi[rows] = high
            sin_lo[rows] = (sin_t - high.astype(jnp.float32)).astype(jnp.bfloat16)
        acc[...] = jnp.zeros_like(acc)

    for j in range(GROUP):
        for c in range(2):
            start = (2 * j + c) * states
            lhs[start : start + states] = coef_ref[c, :, j * PLANE : (j + 1) * PLANE]

    def dot(table, low, cols):
        left = lhs[...]
        return jnp.dot(left, table[:, cols], preferred_element_type=jnp.float32) + jnp.dot(
            left, low[:, cols], preferred_element_type=jnp.float32
        )

    gx = pl.ds(pl.multiple_of(step * GROUP, GROUP), GROUP)
    for m in range(count // chunk):
        cols = slice(m * chunk, (m + 1) * chunk)
        by_cos = dot(cos_hi, cos_lo, cols)
        by_sin = dot(sin_hi, sin_lo, cols)
        pc, ps = xcos[gx, cols], xsin[gx, cols]
        real_sum, imag_sum = acc[0, :, cols], acc[1, :, cols]
        for j in range(GROUP):
            a = slice(2 * j * states, (2 * j + 1) * states)
            b = slice((2 * j + 1) * states, (2 * j + 2) * states)
            re = by_cos[a] - by_sin[b]
            im = by_sin[a] + by_cos[b]
            c, s = pc[j : j + 1], ps[j : j + 1]
            real_sum = real_sum + (re * c - im * s)
            imag_sum = imag_sum + (re * s + im * c)
        acc[0, :, cols] = real_sum
        acc[1, :, cols] = imag_sum

    @pl.when(step == pl.num_programs(0) - 1)
    def _():
        blocks, _, _, length = out_ref.shape
        for b in range(blocks):
            out_ref[b] = acc[:, :, b * length : (b + 1) * length].astype(jnp.bfloat16)


def orbitals_at(coefficients, points, count, length):
    states = coefficients.shape[1]
    total = points.shape[0]
    chunk = 256 if count % 256 == 0 else 128
    table = pltpu.VMEM((PLANE, count), jnp.bfloat16)
    out_shape = (count // length, 2, states, length)
    return pl.pallas_call(
        functools.partial(orbital_kernel, chunk),
        grid=(NG // GROUP,),
        out_shape=jax.ShapeDtypeStruct(out_shape, jnp.bfloat16),
        in_specs=[
            pl.BlockSpec((1, total), lambda i: (0, 0)),
            pl.BlockSpec((2, states, GROUP * PLANE), lambda i: (0, 0, i)),
        ],
        out_specs=pl.BlockSpec(out_shape, lambda i: (0, 0, 0, 0)),
        scratch_shapes=[
            pltpu.VMEM((GROUP * 2 * states, PLANE), jnp.bfloat16),
            table, table, table, table,
            pltpu.VMEM((NG, count), jnp.float32),
            pltpu.VMEM((NG, count), jnp.float32),
            pltpu.VMEM((2, states, count), jnp.float32),
        ],
        compiler_params=pltpu.CompilerParams(vmem_limit_bytes=VMEM_LIMIT),
        name="orbitals",
    )(points.reshape(1, total), coefficients)


def exchange_kernel(groups, n, own_ref, rows, cols, blocks, local_sem, x_send, x_recv,
                    r1_send, r1_recv, c1_send, c1_recv, r2_send, r2_recv,
                    up_send, up_recv, down_send, down_recv):
    me = lax.axis_index("ka")
    g = lax.axis_index("grp")
    line, place = me // n, me % n
    held = own_ref.shape[0]

    def turn(value, by):
        return (value + by) % n

    barrier = pltpu.get_barrier_semaphore()
    for d in range(1, groups):
        pl.semaphore_signal(barrier, inc=1, device_id={"grp": (g + d) % groups, "ka": me},
                            device_id_type=pl.DeviceIdType.MESH)
    for d in range(1, n):
        for peer in (turn(line, d) * n + place, line * n + turn(place, d)):
            pl.semaphore_signal(barrier, inc=1, device_id={"grp": g, "ka": peer},
                                device_id_type=pl.DeviceIdType.MESH)
    pl.semaphore_wait(barrier, groups - 1 + 2 * (n - 1))

    pending = []

    def send(src, dst, send_sem, recv_sem, peer, grp=None, when=None):
        copy = pltpu.make_async_remote_copy(
            src_ref=src, dst_ref=dst, send_sem=send_sem, recv_sem=recv_sem,
            device_id={"grp": g if grp is None else grp, "ka": peer},
            device_id_type=pl.DeviceIdType.MESH,
        )
        guarded(when, copy.start)
        pending.append((when, copy.wait_send))

    def arrive(dst, send_sem, recv_sem):
        pltpu.make_async_remote_copy(
            src_ref=dst, dst_ref=dst, send_sem=send_sem, recv_sem=recv_sem,
            device_id={"grp": g, "ka": turn(line, 1) * n + place},
            device_id_type=pl.DeviceIdType.MESH,
        ).wait_recv()

    def guarded(when, run):
        if when is None:
            run()
        else:
            pl.when(when)(run)

    def share(grp):
        return blocks.at[pl.ds(grp * held, held)]

    for d in range(1, groups):
        send(own_ref, share(g), x_send.at[d], x_recv.at[d], me, grp=(g + d) % groups)
    keep = pltpu.make_async_copy(own_ref, share(g), local_sem.at[0])
    keep.start()
    keep.wait()
    for d in range(1, groups):
        arrive(share((g + groups - d) % groups), x_send.at[d], x_recv.at[d])

    for d in range(1, n):
        send(blocks.at[turn(line, d)], rows.at[me], r1_send.at[d], r1_recv.at[d],
             turn(line, d) * n + place)
        send(blocks.at[turn(place, d)], cols.at[me], c1_send.at[d], c1_recv.at[d],
             line * n + turn(place, d))
    own_row = pltpu.make_async_copy(blocks.at[line], rows.at[me], local_sem.at[1])
    own_col = pltpu.make_async_copy(blocks.at[place], cols.at[me], local_sem.at[2])
    own_row.start()
    own_col.start()

    above, below = line < n - 1, line > 0
    for d in range(n):
        slot = line * n + turn(place, n - d)
        if d:
            arrive(cols.at[slot], c1_send.at[d], c1_recv.at[d])
        source = cols.at[slot] if d else blocks.at[place]
        send(source, cols.at[slot], up_send.at[0, d], up_recv.at[0, d], me + n, when=above)
        send(source, cols.at[slot], down_send.at[0, d], down_recv.at[0, d], me - n, when=below)
        slot = turn(line, n - d) * n + place
        if d:
            arrive(rows.at[slot], r1_send.at[d], r1_recv.at[d])
        source = rows.at[slot] if d else blocks.at[line]
        for e in range(1, n):
            send(source, rows.at[slot], r2_send.at[d, e], r2_recv.at[d, e],
                 line * n + turn(place, e))

    for t in range(1, n):
        for d in range(n):
            def from_below(t=t, d=d):
                slot = (line - t) * n + turn(place, n - d)
                arrive(cols.at[slot], up_send.at[t - 1, d], up_recv.at[t - 1, d])

            def from_above(t=t, d=d):
                slot = (line + t) * n + turn(place, n - d)
                arrive(cols.at[slot], down_send.at[t - 1, d], down_recv.at[t - 1, d])

            pl.when(line - t >= 0)(from_below)
            if t < n - 1:
                slot = jnp.maximum(line - t, 0) * n + turn(place, n - d)
                send(cols.at[slot], cols.at[slot], up_send.at[t, d], up_recv.at[t, d], me + n,
                     when=jnp.logical_and(line - t >= 0, above))
            pl.when(line + t < n)(from_above)
            if t < n - 1:
                slot = jnp.minimum(line + t, n - 1) * n + turn(place, n - d)
                send(cols.at[slot], cols.at[slot], down_send.at[t, d], down_recv.at[t, d], me - n,
                     when=jnp.logical_and(line + t < n, below))

    for d in range(n):
        for e in range(1, n):
            slot = turn(line, n - d) * n + turn(place, n - e)
            arrive(rows.at[slot], r2_send.at[d, e], r2_recv.at[d, e])
    own_row.wait()
    own_col.wait()
    for when, wait in pending:
        guarded(when, wait)


def exchange(own, groups, devices, n):
    _, _, states, length = own.shape
    anywhere = pl.BlockSpec(memory_space=pl.ANY)
    side = jax.ShapeDtypeStruct((devices, 2, states, length), jnp.bfloat16)
    sem = pltpu.SemaphoreType.DMA
    rows, cols, _ = pl.pallas_call(
        functools.partial(exchange_kernel, groups, n),
        out_shape=[side, side, jax.ShapeDtypeStruct((n, 2, states, length), jnp.bfloat16)],
        in_specs=[anywhere],
        out_specs=[anywhere] * 3,
        scratch_shapes=[sem((3,)), sem((groups,)), sem((groups,))]
        + [sem((n,))] * 4 + [sem((n, n))] * 6,
        compiler_params=pltpu.CompilerParams(collective_id=0, has_side_effects=True),
        name="exchange",
    )(own)
    return rows, cols


def polar_kernel(partner_ref, row_ref, col_ref, occ_ref, virt_ref, out_ref):
    kpoints, parts, bands, _ = row_ref.shape
    scaling = 1.0 / (bands * bands)
    dims = (((0,), (0,)), ((), ()))

    diagonal = lax.broadcasted_iota(jnp.int32, (bands, bands), 0) == lax.broadcasted_iota(
        jnp.int32, (bands, bands), 1
    )

    def density(k, weight_ref):
        rows = row_ref[k].astype(jnp.float32)
        weight = jnp.where(diagonal, weight_ref[pl.ds(k, 1), :], 0.0)
        weight = jnp.sum(weight, axis=1, keepdims=True)
        weighted = (rows * weight[None]).astype(jnp.bfloat16)
        cols = col_ref[k]
        right = jnp.concatenate([cols[0], cols[1]], axis=0)
        real_left = jnp.concatenate([weighted[0], weighted[1]], axis=0)
        imag_left = jnp.concatenate([weighted[1], -weighted[0]], axis=0)
        return (
            lax.dot_general(real_left, right, dims, preferred_element_type=jnp.float32),
            lax.dot_general(imag_left, right, dims, preferred_element_type=jnp.float32),
        )

    def step(k, carry):
        occ_real, occ_imag = density(k, occ_ref)
        virt_real, virt_imag = density(partner_ref[k], virt_ref)
        out_ref[0, 0] += (occ_real * virt_real + occ_imag * virt_imag) * scaling
        out_ref[1, 0] += (occ_imag * virt_real - occ_real * virt_imag) * scaling
        return carry

    out_ref[...] = jnp.zeros_like(out_ref)
    lax.fori_loop(0, kpoints, step, 0)


def polarizability(partner, row_side, col_side, occ_weight, virt_weight):
    row_len, col_len = row_side.shape[3], col_side.shape[3]
    vmem = pl.BlockSpec(memory_space=pltpu.VMEM)
    return pl.pallas_call(
        polar_kernel,
        out_shape=jax.ShapeDtypeStruct((2, 1, row_len, col_len), jnp.float32),
        in_specs=[pl.BlockSpec(memory_space=pltpu.SMEM), vmem, vmem, vmem, vmem],
        out_specs=vmem,
        compiler_params=pltpu.CompilerParams(vmem_limit_bytes=VMEM_LIMIT),
        name="polarizability",
    )(partner, row_side, col_side, occ_weight, virt_weight)


def body(coefficients, occ_weight, virt_weight, partner, points):
    devices = lax.axis_size("ka")
    groups = lax.axis_size("grp")
    col_blocks = min(16, max(4, devices // 8))
    row_blocks = devices // col_blocks
    kpoints, bands = occ_weight.shape
    point_count = points.shape[0]
    states = coefficients.shape[1]
    row_len = point_count // row_blocks
    col_len = point_count // col_blocks
    own = orbitals_at(coefficients, points, point_count // groups, row_len)
    rows, cols = exchange(own, groups, devices, col_blocks)

    def by_kpoint(side, length):
        side = side.reshape(kpoints, devices // kpoints, 2, states, length)
        return jnp.swapaxes(side, 1, 2).reshape(kpoints, 2, bands, length)

    return polarizability(
        partner, by_kpoint(rows, row_len), by_kpoint(cols, col_len), occ_weight, virt_weight
    )


def solution(mesh):
    return jax.shard_map(
        body,
        mesh=mesh,
        in_specs=(P(None, "ka", None), P(), P(), P("grp"), P()),
        out_specs=P("grp", "ka", None, None),
        check_vma=False,
    )
```

```python
import functools
import math

import jax
import jax.numpy as jnp
from jax import lax
from jax.experimental import pallas as pl
from jax.experimental.pallas import tpu as pltpu
from jax.sharding import PartitionSpec as P

NG = 32
PLANE = NG * NG
GROUP = 8
VMEM_LIMIT = 56 * 1024 * 1024


def cosine(phase):
    folded = jnp.minimum(phase, NG - phase) - NG // 4
    angle = folded.astype(jnp.float32) * (-2.0 * math.pi / NG)
    square = angle * angle
    total = jnp.full_like(square, 1.0 / math.factorial(13))
    for order in range(11, 0, -2):
        total = (-1.0) ** (order // 2) / math.factorial(order) + square * total
    return angle * total


def phase_rows(frequency, targets):
    phase = frequency * targets
    return cosine(phase & (NG - 1)), cosine((phase - NG // 4) & (NG - 1))


def orbital_kernel(chunk, pts_ref, coef_ref, out_ref, lhs, cos_table, sin_table, xcos, xsin, acc):
    step = pl.program_id(0)
    states = coef_ref.shape[1]
    count = acc.shape[2]

    @pl.when(step == 0)
    def _():
        start = pl.multiple_of(lax.axis_index("grp") * count, 128)
        pts = pts_ref[:, pl.ds(start, count)]
        frequency = lax.broadcasted_iota(jnp.int32, (NG, count), 0)
        norm = 1.0 / math.sqrt(NG**3)
        cos_x, sin_x = phase_rows(frequency, pts >> 10)
        xcos[...] = cos_x * norm
        xsin[...] = sin_x * norm
        cos_y, sin_y = phase_rows(frequency, (pts >> 5) & (NG - 1))
        cos_z, sin_z = phase_rows(frequency, pts & (NG - 1))
        for gy in range(NG):
            rows = slice(gy * NG, (gy + 1) * NG)
            cy, sy = cos_y[gy : gy + 1], sin_y[gy : gy + 1]
            cos_t = cy * cos_z - sy * sin_z
            sin_t = sy * cos_z + cy * sin_z
            low_rows = slice(PLANE + gy * NG, PLANE + (gy + 1) * NG)
            for table, value in ((cos_table, cos_t), (sin_table, sin_t)):
                high = value.astype(jnp.bfloat16)
                table[rows] = high
                table[low_rows] = (value - high.astype(jnp.float32)).astype(jnp.bfloat16)
        acc[...] = jnp.zeros_like(acc)

    for j in range(GROUP):
        for c in range(2):
            start = (2 * j + c) * states
            value = coef_ref[c, :, j * PLANE : (j + 1) * PLANE]
            lhs[start : start + states, :PLANE] = value
            lhs[start : start + states, PLANE:] = value

    def dot(table, cols):
        return jnp.dot(lhs[...], table[:, cols], preferred_element_type=jnp.float32)

    gx = pl.ds(pl.multiple_of(step * GROUP, GROUP), GROUP)
    for m in range(count // chunk):
        cols = slice(m * chunk, (m + 1) * chunk)
        by_cos = dot(cos_table, cols)
        by_sin = dot(sin_table, cols)
        pc, ps = xcos[gx, cols], xsin[gx, cols]
        real_sum, imag_sum = acc[0, :, cols], acc[1, :, cols]
        for j in range(GROUP):
            a = slice(2 * j * states, (2 * j + 1) * states)
            b = slice((2 * j + 1) * states, (2 * j + 2) * states)
            re = by_cos[a] - by_sin[b]
            im = by_sin[a] + by_cos[b]
            c, s = pc[j : j + 1], ps[j : j + 1]
            real_sum = real_sum + (re * c - im * s)
            imag_sum = imag_sum + (re * s + im * c)
        acc[0, :, cols] = real_sum
        acc[1, :, cols] = imag_sum

    @pl.when(step == pl.num_programs(0) - 1)
    def _():
        blocks, _, _, length = out_ref.shape
        for b in range(blocks):
            out_ref[b] = acc[:, :, b * length : (b + 1) * length].astype(jnp.bfloat16)


def orbitals_at(coefficients, points, count, length):
    states = coefficients.shape[1]
    total = points.shape[0]
    chunk = 256 if count % 256 == 0 else 128
    table = pltpu.VMEM((2 * PLANE, count), jnp.bfloat16)
    out_shape = (count // length, 2, states, length)
    return pl.pallas_call(
        functools.partial(orbital_kernel, chunk),
        grid=(NG // GROUP,),
        out_shape=jax.ShapeDtypeStruct(out_shape, jnp.bfloat16),
        in_specs=[
            pl.BlockSpec((1, total), lambda i: (0, 0)),
            pl.BlockSpec((2, states, GROUP * PLANE), lambda i: (0, 0, i)),
        ],
        out_specs=pl.BlockSpec(out_shape, lambda i: (0, 0, 0, 0)),
        scratch_shapes=[
            pltpu.VMEM((GROUP * 2 * states, 2 * PLANE), jnp.bfloat16),
            table, table,
            pltpu.VMEM((NG, count), jnp.float32),
            pltpu.VMEM((NG, count), jnp.float32),
            pltpu.VMEM((2, states, count), jnp.float32),
        ],
        compiler_params=pltpu.CompilerParams(vmem_limit_bytes=VMEM_LIMIT),
        name="orbitals",
    )(points.reshape(1, total), coefficients)


def exchange_kernel(groups, n, own_ref, rows, cols, blocks, local_sem, x_send, x_recv,
                    r1_send, r1_recv, c1_send, c1_recv, r2_send, r2_recv,
                    up_send, up_recv, down_send, down_recv):
    me = lax.axis_index("ka")
    g = lax.axis_index("grp")
    line, place = me // n, me % n
    held = own_ref.shape[0]

    def turn(value, by):
        return (value + by) % n

    barrier = pltpu.get_barrier_semaphore()
    for d in range(1, groups):
        pl.semaphore_signal(barrier, inc=1, device_id={"grp": (g + d) % groups, "ka": me},
                            device_id_type=pl.DeviceIdType.MESH)
    for d in range(1, n):
        for peer in (turn(line, d) * n + place, line * n + turn(place, d)):
            pl.semaphore_signal(barrier, inc=1, device_id={"grp": g, "ka": peer},
                                device_id_type=pl.DeviceIdType.MESH)
    pl.semaphore_wait(barrier, groups - 1 + 2 * (n - 1))

    pending = []

    def send(src, dst, send_sem, recv_sem, peer, grp=None, when=None):
        copy = pltpu.make_async_remote_copy(
            src_ref=src, dst_ref=dst, send_sem=send_sem, recv_sem=recv_sem,
            device_id={"grp": g if grp is None else grp, "ka": peer},
            device_id_type=pl.DeviceIdType.MESH,
        )
        guarded(when, copy.start)
        pending.append((when, copy.wait_send))

    def arrive(dst, send_sem, recv_sem):
        pltpu.make_async_remote_copy(
            src_ref=dst, dst_ref=dst, send_sem=send_sem, recv_sem=recv_sem,
            device_id={"grp": g, "ka": turn(line, 1) * n + place},
            device_id_type=pl.DeviceIdType.MESH,
        ).wait_recv()

    def guarded(when, run):
        if when is None:
            run()
        else:
            pl.when(when)(run)

    def share(grp):
        return blocks.at[pl.ds(grp * held, held)]

    for d in range(1, groups):
        send(own_ref, share(g), x_send.at[d], x_recv.at[d], me, grp=(g + d) % groups)
    keep = pltpu.make_async_copy(own_ref, share(g), local_sem.at[0])
    keep.start()
    keep.wait()
    for d in range(1, groups):
        arrive(share((g + groups - d) % groups), x_send.at[d], x_recv.at[d])

    for d in range(1, n):
        send(blocks.at[turn(line, d)], rows.at[me], r1_send.at[d], r1_recv.at[d],
             turn(line, d) * n + place)
        send(blocks.at[turn(place, d)], cols.at[me], c1_send.at[d], c1_recv.at[d],
             line * n + turn(place, d))
    own_row = pltpu.make_async_copy(blocks.at[line], rows.at[me], local_sem.at[1])
    own_col = pltpu.make_async_copy(blocks.at[place], cols.at[me], local_sem.at[2])
    own_row.start()
    own_col.start()

    above, below = line < n - 1, line > 0
    for d in range(n):
        slot = line * n + turn(place, n - d)
        if d:
            arrive(cols.at[slot], c1_send.at[d], c1_recv.at[d])
        source = cols.at[slot] if d else blocks.at[place]
        send(source, cols.at[slot], up_send.at[0, d], up_recv.at[0, d], me + n, when=above)
        send(source, cols.at[slot], down_send.at[0, d], down_recv.at[0, d], me - n, when=below)
        slot = turn(line, n - d) * n + place
        if d:
            arrive(rows.at[slot], r1_send.at[d], r1_recv.at[d])
        source = rows.at[slot] if d else blocks.at[line]
        for e in range(1, n):
            send(source, rows.at[slot], r2_send.at[d, e], r2_recv.at[d, e],
                 line * n + turn(place, e))

    for t in range(1, n):
        for d in range(n):
            def from_below(t=t, d=d):
                slot = (line - t) * n + turn(place, n - d)
                arrive(cols.at[slot], up_send.at[t - 1, d], up_recv.at[t - 1, d])

            def from_above(t=t, d=d):
                slot = (line + t) * n + turn(place, n - d)
                arrive(cols.at[slot], down_send.at[t - 1, d], down_recv.at[t - 1, d])

            pl.when(line - t >= 0)(from_below)
            if t < n - 1:
                slot = jnp.maximum(line - t, 0) * n + turn(place, n - d)
                send(cols.at[slot], cols.at[slot], up_send.at[t, d], up_recv.at[t, d], me + n,
                     when=jnp.logical_and(line - t >= 0, above))
            pl.when(line + t < n)(from_above)
            if t < n - 1:
                slot = jnp.minimum(line + t, n - 1) * n + turn(place, n - d)
                send(cols.at[slot], cols.at[slot], down_send.at[t, d], down_recv.at[t, d], me - n,
                     when=jnp.logical_and(line + t < n, below))

    for d in range(n):
        for e in range(1, n):
            slot = turn(line, n - d) * n + turn(place, n - e)
            arrive(rows.at[slot], r2_send.at[d, e], r2_recv.at[d, e])
    own_row.wait()
    own_col.wait()
    for when, wait in pending:
        guarded(when, wait)


def exchange(own, groups, devices, n):
    _, _, states, length = own.shape
    anywhere = pl.BlockSpec(memory_space=pl.ANY)
    side = jax.ShapeDtypeStruct((devices, 2, states, length), jnp.bfloat16)
    sem = pltpu.SemaphoreType.DMA
    rows, cols, _ = pl.pallas_call(
        functools.partial(exchange_kernel, groups, n),
        out_shape=[side, side, jax.ShapeDtypeStruct((n, 2, states, length), jnp.bfloat16)],
        in_specs=[anywhere],
        out_specs=[anywhere] * 3,
        scratch_shapes=[sem((3,)), sem((groups,)), sem((groups,))]
        + [sem((n,))] * 4 + [sem((n, n))] * 6,
        compiler_params=pltpu.CompilerParams(collective_id=0, has_side_effects=True),
        name="exchange",
    )(own)
    return rows, cols


def polar_kernel(partner_ref, row_ref, col_ref, occ_ref, virt_ref, out_ref, right_ref, acc):
    kpoints, parts, bands, row_len = row_ref.shape
    col_len = col_ref.shape[3]
    tile = col_len // 3 if col_len % 384 == 0 else col_len
    scaling = 1.0 / (bands * bands)
    diagonal = lax.broadcasted_iota(jnp.int32, (bands, bands), 0) == lax.broadcasted_iota(
        jnp.int32, (bands, bands), 1
    )

    def left(k, weight_ref):
        weight = jnp.where(diagonal, weight_ref[pl.ds(k, 1), :], 0.0)
        weight = jnp.sum(weight, axis=1, keepdims=True)
        weighted = (row_ref[k].astype(jnp.float32) * weight[None]).astype(jnp.bfloat16)
        real, imag = weighted[0], weighted[1]
        return jnp.concatenate([real, imag], axis=0), jnp.concatenate([imag, -real], axis=0)

    def turn(k, carry):
        cols = col_ref[k]
        right_ref[k] = jnp.concatenate([cols[0], cols[1]], axis=0).T
        return carry

    def step(k, carry):
        other = partner_ref[k]
        occ_left = left(k, occ_ref)
        virt_left = left(other, virt_ref)
        for m in range(col_len // tile):
            rows = slice(m * tile, (m + 1) * tile)
            occ_right, virt_right = right_ref[k, rows], right_ref[other, rows]
            occ_real, occ_imag = [
                jnp.dot(occ_right, value, preferred_element_type=jnp.float32) for value in occ_left
            ]
            virt_real, virt_imag = [
                jnp.dot(virt_right, value, preferred_element_type=jnp.float32) for value in virt_left
            ]
            acc[0, rows] += occ_real * virt_real + occ_imag * virt_imag
            acc[1, rows] += occ_imag * virt_real - occ_real * virt_imag
        return carry

    acc[...] = jnp.zeros_like(acc)
    lax.fori_loop(0, kpoints, turn, 0)
    lax.fori_loop(0, kpoints, step, 0)
    for c in range(parts):
        out_ref[c, 0] = acc[c].T * scaling


def polarizability(partner, row_side, col_side, occ_weight, virt_weight):
    row_len, col_len = row_side.shape[3], col_side.shape[3]
    vmem = pl.BlockSpec(memory_space=pltpu.VMEM)
    return pl.pallas_call(
        polar_kernel,
        out_shape=jax.ShapeDtypeStruct((2, 1, row_len, col_len), jnp.float32),
        in_specs=[pl.BlockSpec(memory_space=pltpu.SMEM), vmem, vmem, vmem, vmem],
        out_specs=vmem,
        scratch_shapes=[
            pltpu.VMEM((col_side.shape[0], col_len, 2 * col_side.shape[2]), jnp.bfloat16),
            pltpu.VMEM((2, col_len, row_len), jnp.float32),
        ],
        compiler_params=pltpu.CompilerParams(vmem_limit_bytes=VMEM_LIMIT),
        name="polarizability",
    )(partner, row_side, col_side, occ_weight, virt_weight)


def body(coefficients, occ_weight, virt_weight, partner, points):
    devices = lax.axis_size("ka")
    groups = lax.axis_size("grp")
    col_blocks = min(16, max(4, devices // 8))
    row_blocks = devices // col_blocks
    kpoints, bands = occ_weight.shape
    point_count = points.shape[0]
    states = coefficients.shape[1]
    row_len = point_count // row_blocks
    col_len = point_count // col_blocks
    own = orbitals_at(coefficients, points, point_count // groups, row_len)
    rows, cols = exchange(own, groups, devices, col_blocks)

    def by_kpoint(side, length):
        side = side.reshape(kpoints, devices // kpoints, 2, states, length)
        return jnp.swapaxes(side, 1, 2).reshape(kpoints, 2, bands, length)

    return polarizability(
        partner, by_kpoint(rows, row_len), by_kpoint(cols, col_len), occ_weight, virt_weight
    )


def solution(mesh):
    return jax.shard_map(
        body,
        mesh=mesh,
        in_specs=(P(None, "ka", None), P(), P(), P("grp"), P()),
        out_specs=P("grp", "ka", None, None),
        check_vma=False,
    )
```

```python
import functools
import math

import jax
import jax.numpy as jnp
from jax import lax
from jax.experimental import pallas as pl
from jax.experimental.pallas import tpu as pltpu
from jax.sharding import PartitionSpec as P

NG = 32
PLANE = NG * NG
GROUP = 8
VMEM_LIMIT = 56 * 1024 * 1024


def cosine(phase):
    folded = jnp.minimum(phase, NG - phase) - NG // 4
    angle = folded.astype(jnp.float32) * (-2.0 * math.pi / NG)
    square = angle * angle
    total = jnp.full_like(square, 1.0 / math.factorial(13))
    for order in range(11, 0, -2):
        total = (-1.0) ** (order // 2) / math.factorial(order) + square * total
    return angle * total


def phase_rows(frequency, targets):
    phase = frequency * targets
    return cosine(phase & (NG - 1)), cosine((phase - NG // 4) & (NG - 1))


def orbital_kernel(chunk, pts_ref, coef_ref, out_ref, lhs, cos_table, sin_table, xcos, xsin, acc):
    step = pl.program_id(0)
    states = coef_ref.shape[1]
    count = acc.shape[2]

    @pl.when(step == 0)
    def _():
        start = pl.multiple_of(lax.axis_index("grp") * count, 128)
        pts = pts_ref[:, pl.ds(start, count)]
        frequency = lax.broadcasted_iota(jnp.int32, (NG, count), 0)
        norm = 1.0 / math.sqrt(NG**3)
        cos_x, sin_x = phase_rows(frequency, pts >> 10)
        xcos[...] = cos_x * norm
        xsin[...] = sin_x * norm
        cos_y, sin_y = phase_rows(frequency, (pts >> 5) & (NG - 1))
        cos_z, sin_z = phase_rows(frequency, pts & (NG - 1))
        for gy in range(NG):
            rows = slice(gy * NG, (gy + 1) * NG)
            cy, sy = cos_y[gy : gy + 1], sin_y[gy : gy + 1]
            cos_t = cy * cos_z - sy * sin_z
            sin_t = sy * cos_z + cy * sin_z
            low_rows = slice(PLANE + gy * NG, PLANE + (gy + 1) * NG)
            for table, value in ((cos_table, cos_t), (sin_table, sin_t)):
                high = value.astype(jnp.bfloat16)
                table[rows] = high
                table[low_rows] = (value - high.astype(jnp.float32)).astype(jnp.bfloat16)
        acc[...] = jnp.zeros_like(acc)

    for j in range(GROUP):
        for c in range(2):
            start = (2 * j + c) * states
            value = coef_ref[c, :, j * PLANE : (j + 1) * PLANE]
            lhs[start : start + states, :PLANE] = value
            lhs[start : start + states, PLANE:] = value

    def dot(table, cols):
        return jnp.dot(lhs[...], table[:, cols], preferred_element_type=jnp.float32)

    gx = pl.ds(pl.multiple_of(step * GROUP, GROUP), GROUP)
    for m in range(count // chunk):
        cols = slice(m * chunk, (m + 1) * chunk)
        by_cos = dot(cos_table, cols)
        by_sin = dot(sin_table, cols)
        pc, ps = xcos[gx, cols], xsin[gx, cols]
        real_sum, imag_sum = acc[0, :, cols], acc[1, :, cols]
        for j in range(GROUP):
            a = slice(2 * j * states, (2 * j + 1) * states)
            b = slice((2 * j + 1) * states, (2 * j + 2) * states)
            re = by_cos[a] - by_sin[b]
            im = by_sin[a] + by_cos[b]
            c, s = pc[j : j + 1], ps[j : j + 1]
            real_sum = real_sum + (re * c - im * s)
            imag_sum = imag_sum + (re * s + im * c)
        acc[0, :, cols] = real_sum
        acc[1, :, cols] = imag_sum

    @pl.when(step == pl.num_programs(0) - 1)
    def _():
        blocks, _, _, length = out_ref.shape
        for b in range(blocks):
            out_ref[b] = acc[:, :, b * length : (b + 1) * length].astype(jnp.bfloat16)


def orbitals_at(coefficients, points, count, length):
    states = coefficients.shape[1]
    total = points.shape[0]
    chunk = 256 if count % 256 == 0 else 128
    table = pltpu.VMEM((2 * PLANE, count), jnp.bfloat16)
    out_shape = (count // length, 2, states, length)
    return pl.pallas_call(
        functools.partial(orbital_kernel, chunk),
        grid=(NG // GROUP,),
        out_shape=jax.ShapeDtypeStruct(out_shape, jnp.bfloat16),
        in_specs=[
            pl.BlockSpec((1, total), lambda i: (0, 0)),
            pl.BlockSpec((2, states, GROUP * PLANE), lambda i: (0, 0, i)),
        ],
        out_specs=pl.BlockSpec(out_shape, lambda i: (0, 0, 0, 0)),
        scratch_shapes=[
            pltpu.VMEM((GROUP * 2 * states, 2 * PLANE), jnp.bfloat16),
            table, table,
            pltpu.VMEM((NG, count), jnp.float32),
            pltpu.VMEM((NG, count), jnp.float32),
            pltpu.VMEM((2, states, count), jnp.float32),
        ],
        compiler_params=pltpu.CompilerParams(vmem_limit_bytes=VMEM_LIMIT),
        name="orbitals",
    )(points.reshape(1, total), coefficients)


def exchange_kernel(groups, n, own_ref, rows, cols, blocks, local_sem, x_send, x_recv,
                    r1_send, r1_recv, c1_send, c1_recv, r2_send, r2_recv,
                    up_send, up_recv, down_send, down_recv):
    me = lax.axis_index("ka")
    g = lax.axis_index("grp")
    line, place = me // n, me % n
    held = own_ref.shape[0]

    def turn(value, by):
        return (value + by) % n

    barrier = pltpu.get_barrier_semaphore()
    for d in range(1, groups):
        pl.semaphore_signal(barrier, inc=1, device_id={"grp": (g + d) % groups, "ka": me},
                            device_id_type=pl.DeviceIdType.MESH)
    for d in range(1, n):
        for peer in (turn(line, d) * n + place, line * n + turn(place, d)):
            pl.semaphore_signal(barrier, inc=1, device_id={"grp": g, "ka": peer},
                                device_id_type=pl.DeviceIdType.MESH)
    pl.semaphore_wait(barrier, groups - 1 + 2 * (n - 1))

    pending = []

    def send(src, dst, send_sem, recv_sem, peer, grp=None, when=None):
        copy = pltpu.make_async_remote_copy(
            src_ref=src, dst_ref=dst, send_sem=send_sem, recv_sem=recv_sem,
            device_id={"grp": g if grp is None else grp, "ka": peer},
            device_id_type=pl.DeviceIdType.MESH,
        )
        guarded(when, copy.start)
        pending.append((when, copy.wait_send))

    def arrive(dst, send_sem, recv_sem):
        pltpu.make_async_remote_copy(
            src_ref=dst, dst_ref=dst, send_sem=send_sem, recv_sem=recv_sem,
            device_id={"grp": g, "ka": turn(line, 1) * n + place},
            device_id_type=pl.DeviceIdType.MESH,
        ).wait_recv()

    def guarded(when, run):
        if when is None:
            run()
        else:
            pl.when(when)(run)

    def share(grp):
        return blocks.at[pl.ds(grp * held, held)]

    for d in range(1, groups):
        send(own_ref, share(g), x_send.at[d], x_recv.at[d], me, grp=(g + d) % groups)
    keep = pltpu.make_async_copy(own_ref, share(g), local_sem.at[0])
    keep.start()
    keep.wait()
    for d in range(1, groups):
        arrive(share((g + groups - d) % groups), x_send.at[d], x_recv.at[d])

    for d in range(1, n):
        send(blocks.at[turn(line, d)], rows.at[me], r1_send.at[d], r1_recv.at[d],
             turn(line, d) * n + place)
        send(blocks.at[turn(place, d)], cols.at[me], c1_send.at[d], c1_recv.at[d],
             line * n + turn(place, d))
    own_row = pltpu.make_async_copy(blocks.at[line], rows.at[me], local_sem.at[1])
    own_col = pltpu.make_async_copy(blocks.at[place], cols.at[me], local_sem.at[2])
    own_row.start()
    own_col.start()

    above, below = line < n - 1, line > 0
    for d in range(n):
        slot = line * n + turn(place, n - d)
        if d:
            arrive(cols.at[slot], c1_send.at[d], c1_recv.at[d])
        source = cols.at[slot] if d else blocks.at[place]
        send(source, cols.at[slot], up_send.at[0, d], up_recv.at[0, d], me + n, when=above)
        send(source, cols.at[slot], down_send.at[0, d], down_recv.at[0, d], me - n, when=below)
        slot = turn(line, n - d) * n + place
        if d:
            arrive(rows.at[slot], r1_send.at[d], r1_recv.at[d])
        source = rows.at[slot] if d else blocks.at[line]
        for e in range(1, n):
            send(source, rows.at[slot], r2_send.at[d, e], r2_recv.at[d, e],
                 line * n + turn(place, e))

    for t in range(1, n):
        for d in range(n):
            def from_below(t=t, d=d):
                slot = (line - t) * n + turn(place, n - d)
                arrive(cols.at[slot], up_send.at[t - 1, d], up_recv.at[t - 1, d])

            def from_above(t=t, d=d):
                slot = (line + t) * n + turn(place, n - d)
                arrive(cols.at[slot], down_send.at[t - 1, d], down_recv.at[t - 1, d])

            pl.when(line - t >= 0)(from_below)
            if t < n - 1:
                slot = jnp.maximum(line - t, 0) * n + turn(place, n - d)
                send(cols.at[slot], cols.at[slot], up_send.at[t, d], up_recv.at[t, d], me + n,
                     when=jnp.logical_and(line - t >= 0, above))
            pl.when(line + t < n)(from_above)
            if t < n - 1:
                slot = jnp.minimum(line + t, n - 1) * n + turn(place, n - d)
                send(cols.at[slot], cols.at[slot], down_send.at[t, d], down_recv.at[t, d], me - n,
                     when=jnp.logical_and(line + t < n, below))

    for d in range(n):
        for e in range(1, n):
            slot = turn(line, n - d) * n + turn(place, n - e)
            arrive(rows.at[slot], r2_send.at[d, e], r2_recv.at[d, e])
    own_row.wait()
    own_col.wait()
    for when, wait in pending:
        guarded(when, wait)


def exchange(own, groups, devices, n):
    _, _, states, length = own.shape
    inside = pl.BlockSpec(memory_space=pltpu.VMEM)
    side = jax.ShapeDtypeStruct((devices, 2, states, length), jnp.bfloat16)
    sem = pltpu.SemaphoreType.DMA
    rows, cols, _ = pl.pallas_call(
        functools.partial(exchange_kernel, groups, n),
        out_shape=[side, side, jax.ShapeDtypeStruct((n, 2, states, length), jnp.bfloat16)],
        in_specs=[inside],
        out_specs=[inside] * 3,
        scratch_shapes=[sem((3,)), sem((groups,)), sem((groups,))]
        + [sem((n,))] * 4 + [sem((n, n))] * 6,
        compiler_params=pltpu.CompilerParams(collective_id=0, has_side_effects=True),
        name="exchange",
    )(own)
    return rows, cols


def polar_kernel(partner_ref, row_ref, col_ref, occ_ref, virt_ref, out_ref, right_ref, acc):
    kpoints, parts, bands, row_len = row_ref.shape
    col_len = col_ref.shape[3]
    tile = col_len // 3 if col_len % 384 == 0 else col_len
    scaling = 1.0 / (bands * bands)
    diagonal = lax.broadcasted_iota(jnp.int32, (bands, bands), 0) == lax.broadcasted_iota(
        jnp.int32, (bands, bands), 1
    )

    def left(k, weight_ref):
        weight = jnp.where(diagonal, weight_ref[pl.ds(k, 1), :], 0.0)
        weight = jnp.sum(weight, axis=1, keepdims=True)
        weighted = (row_ref[k].astype(jnp.float32) * weight[None]).astype(jnp.bfloat16)
        real, imag = weighted[0], weighted[1]
        return jnp.concatenate([real, imag], axis=0), jnp.concatenate([imag, -real], axis=0)

    def turn(k, carry):
        cols = col_ref[k]
        right_ref[k] = jnp.concatenate([cols[0], cols[1]], axis=0).T
        return carry

    def step(k, carry):
        other = partner_ref[k]
        occ_left = left(k, occ_ref)
        virt_left = left(other, virt_ref)
        for m in range(col_len // tile):
            rows = slice(m * tile, (m + 1) * tile)
            occ_right, virt_right = right_ref[k, rows], right_ref[other, rows]
            occ_real, occ_imag = [
                jnp.dot(occ_right, value, preferred_element_type=jnp.float32) for value in occ_left
            ]
            virt_real, virt_imag = [
                jnp.dot(virt_right, value, preferred_element_type=jnp.float32) for value in virt_left
            ]
            acc[0, rows] += occ_real * virt_real + occ_imag * virt_imag
            acc[1, rows] += occ_imag * virt_real - occ_real * virt_imag
        return carry

    acc[...] = jnp.zeros_like(acc)
    lax.fori_loop(0, kpoints, turn, 0)
    lax.fori_loop(0, kpoints, step, 0)
    for c in range(parts):
        out_ref[c, 0] = acc[c].T * scaling


def polarizability(partner, row_side, col_side, occ_weight, virt_weight):
    row_len, col_len = row_side.shape[3], col_side.shape[3]
    vmem = pl.BlockSpec(memory_space=pltpu.VMEM)
    return pl.pallas_call(
        polar_kernel,
        out_shape=jax.ShapeDtypeStruct((2, 1, row_len, col_len), jnp.float32),
        in_specs=[pl.BlockSpec(memory_space=pltpu.SMEM), vmem, vmem, vmem, vmem],
        out_specs=vmem,
        scratch_shapes=[
            pltpu.VMEM((col_side.shape[0], col_len, 2 * col_side.shape[2]), jnp.bfloat16),
            pltpu.VMEM((2, col_len, row_len), jnp.float32),
        ],
        compiler_params=pltpu.CompilerParams(vmem_limit_bytes=VMEM_LIMIT),
        name="polarizability",
    )(partner, row_side, col_side, occ_weight, virt_weight)


def body(coefficients, occ_weight, virt_weight, partner, points):
    devices = lax.axis_size("ka")
    groups = lax.axis_size("grp")
    col_blocks = min(16, max(4, devices // 8))
    row_blocks = devices // col_blocks
    kpoints, bands = occ_weight.shape
    point_count = points.shape[0]
    states = coefficients.shape[1]
    row_len = point_count // row_blocks
    col_len = point_count // col_blocks
    own = orbitals_at(coefficients, points, point_count // groups, row_len)
    rows, cols = exchange(own, groups, devices, col_blocks)

    def by_kpoint(side, length):
        side = side.reshape(kpoints, devices // kpoints, 2, states, length)
        return jnp.swapaxes(side, 1, 2).reshape(kpoints, 2, bands, length)

    return polarizability(
        partner, by_kpoint(rows, row_len), by_kpoint(cols, col_len), occ_weight, virt_weight
    )


def solution(mesh):
    return jax.shard_map(
        body,
        mesh=mesh,
        in_specs=(P(None, "ka", None), P(), P(), P("grp"), P()),
        out_specs=P("grp", "ka", None, None),
        check_vma=False,
    )
```

```python
import functools
import math

import jax
import jax.numpy as jnp
from jax import lax
from jax.experimental import pallas as pl
from jax.experimental.pallas import tpu as pltpu
from jax.sharding import PartitionSpec as P

NG = 32
PLANE = NG * NG
GROUP = 8
VMEM_LIMIT = 56 * 1024 * 1024


def cosine(phase):
    folded = jnp.minimum(phase, NG - phase) - NG // 4
    angle = folded.astype(jnp.float32) * (-2.0 * math.pi / NG)
    square = angle * angle
    total = jnp.full_like(square, 1.0 / math.factorial(13))
    for order in range(11, 0, -2):
        total = (-1.0) ** (order // 2) / math.factorial(order) + square * total
    return angle * total


def phase_rows(frequency, targets):
    phase = frequency * targets
    return cosine(phase & (NG - 1)), cosine((phase - NG // 4) & (NG - 1))


def orbital_kernel(chunk, pts_ref, coef_ref, out_ref, lhs, cos_table, sin_table, xcos, xsin, acc):
    step = pl.program_id(0)
    states = coef_ref.shape[1]
    count = acc.shape[2]

    @pl.when(step == 0)
    def _():
        start = pl.multiple_of(lax.axis_index("grp") * count, 128)
        pts = pts_ref[:, pl.ds(start, count)]
        frequency = lax.broadcasted_iota(jnp.int32, (NG, count), 0)
        norm = 1.0 / math.sqrt(NG**3)
        cos_x, sin_x = phase_rows(frequency, pts >> 10)
        xcos[...] = cos_x * norm
        xsin[...] = sin_x * norm
        cos_y, sin_y = phase_rows(frequency, (pts >> 5) & (NG - 1))
        cos_z, sin_z = phase_rows(frequency, pts & (NG - 1))
        for gy in range(NG):
            rows = slice(gy * NG, (gy + 1) * NG)
            cy, sy = cos_y[gy : gy + 1], sin_y[gy : gy + 1]
            cos_t = cy * cos_z - sy * sin_z
            sin_t = sy * cos_z + cy * sin_z
            low_rows = slice(PLANE + gy * NG, PLANE + (gy + 1) * NG)
            for table, value in ((cos_table, cos_t), (sin_table, sin_t)):
                high = value.astype(jnp.bfloat16)
                table[rows] = high
                table[low_rows] = (value - high.astype(jnp.float32)).astype(jnp.bfloat16)
        acc[...] = jnp.zeros_like(acc)

    for j in range(GROUP):
        for c in range(2):
            start = (2 * j + c) * states
            value = coef_ref[c, :, j * PLANE : (j + 1) * PLANE]
            lhs[start : start + states, :PLANE] = value
            lhs[start : start + states, PLANE:] = value

    def dot(table, cols):
        return jnp.dot(lhs[...], table[:, cols], preferred_element_type=jnp.float32)

    gx = pl.ds(pl.multiple_of(step * GROUP, GROUP), GROUP)
    for m in range(count // chunk):
        cols = slice(m * chunk, (m + 1) * chunk)
        by_cos = dot(cos_table, cols)
        by_sin = dot(sin_table, cols)
        pc, ps = xcos[gx, cols], xsin[gx, cols]
        real_sum, imag_sum = acc[0, :, cols], acc[1, :, cols]
        for j in range(GROUP):
            a = slice(2 * j * states, (2 * j + 1) * states)
            b = slice((2 * j + 1) * states, (2 * j + 2) * states)
            re = by_cos[a] - by_sin[b]
            im = by_sin[a] + by_cos[b]
            c, s = pc[j : j + 1], ps[j : j + 1]
            real_sum = real_sum + (re * c - im * s)
            imag_sum = imag_sum + (re * s + im * c)
        acc[0, :, cols] = real_sum
        acc[1, :, cols] = imag_sum

    @pl.when(step == pl.num_programs(0) - 1)
    def _():
        blocks, _, _, length = out_ref.shape
        for b in range(blocks):
            out_ref[b] = acc[:, :, b * length : (b + 1) * length].astype(jnp.bfloat16)


def orbitals_at(coefficients, points, count, length):
    states = coefficients.shape[1]
    total = points.shape[0]
    chunk = 256 if count % 256 == 0 else 128
    table = pltpu.VMEM((2 * PLANE, count), jnp.bfloat16)
    out_shape = (count // length, 2, states, length)
    return pl.pallas_call(
        functools.partial(orbital_kernel, chunk),
        grid=(NG // GROUP,),
        out_shape=jax.ShapeDtypeStruct(out_shape, jnp.bfloat16),
        in_specs=[
            pl.BlockSpec((1, total), lambda i: (0, 0)),
            pl.BlockSpec((2, states, GROUP * PLANE), lambda i: (0, 0, i)),
        ],
        out_specs=pl.BlockSpec(out_shape, lambda i: (0, 0, 0, 0)),
        scratch_shapes=[
            pltpu.VMEM((GROUP * 2 * states, 2 * PLANE), jnp.bfloat16),
            table, table,
            pltpu.VMEM((NG, count), jnp.float32),
            pltpu.VMEM((NG, count), jnp.float32),
            pltpu.VMEM((2, states, count), jnp.float32),
        ],
        compiler_params=pltpu.CompilerParams(vmem_limit_bytes=VMEM_LIMIT),
        name="orbitals",
    )(points.reshape(1, total), coefficients)


def exchange_kernel(groups, n, own_ref, rows, cols, blocks, local_sem, x_send, x_recv,
                    r1_send, r1_recv, c1_send, c1_recv, r2_send, r2_recv,
                    up_send, up_recv, down_send, down_recv):
    me = lax.axis_index("ka")
    g = lax.axis_index("grp")
    line, place = me // n, me % n
    held = own_ref.shape[0]

    def turn(value, by):
        return (value + by) % n

    barrier = pltpu.get_barrier_semaphore()
    for d in range(1, groups):
        pl.semaphore_signal(barrier, inc=1, device_id={"grp": (g + d) % groups, "ka": me},
                            device_id_type=pl.DeviceIdType.MESH)
    for d in range(1, n):
        for peer in (turn(line, d) * n + place, line * n + turn(place, d)):
            pl.semaphore_signal(barrier, inc=1, device_id={"grp": g, "ka": peer},
                                device_id_type=pl.DeviceIdType.MESH)
    pl.semaphore_wait(barrier, groups - 1 + 2 * (n - 1))

    pending = []

    def send(src, dst, send_sem, recv_sem, peer, grp=None, when=None):
        copy = pltpu.make_async_remote_copy(
            src_ref=src, dst_ref=dst, send_sem=send_sem, recv_sem=recv_sem,
            device_id={"grp": g if grp is None else grp, "ka": peer},
            device_id_type=pl.DeviceIdType.MESH,
        )
        guarded(when, copy.start)
        pending.append((when, copy.wait_send))

    def arrive(dst, send_sem, recv_sem):
        pltpu.make_async_remote_copy(
            src_ref=dst, dst_ref=dst, send_sem=send_sem, recv_sem=recv_sem,
            device_id={"grp": g, "ka": turn(line, 1) * n + place},
            device_id_type=pl.DeviceIdType.MESH,
        ).wait_recv()

    def guarded(when, run):
        if when is None:
            run()
        else:
            pl.when(when)(run)

    def share(grp):
        return blocks.at[pl.ds(grp * held, held)]

    for d in range(1, groups):
        send(own_ref, share(g), x_send.at[d], x_recv.at[d], me, grp=(g + d) % groups)
    keep = pltpu.make_async_copy(own_ref, share(g), local_sem.at[0])
    keep.start()
    keep.wait()
    for d in range(1, groups):
        arrive(share((g + groups - d) % groups), x_send.at[d], x_recv.at[d])

    for d in range(1, n):
        send(blocks.at[turn(line, d)], rows.at[me], r1_send.at[d], r1_recv.at[d],
             turn(line, d) * n + place)
        send(blocks.at[turn(place, d)], cols.at[me], c1_send.at[d], c1_recv.at[d],
             line * n + turn(place, d))
    own_row = pltpu.make_async_copy(blocks.at[line], rows.at[me], local_sem.at[1])
    own_col = pltpu.make_async_copy(blocks.at[place], cols.at[me], local_sem.at[2])
    own_row.start()
    own_col.start()

    above, below = line < n - 1, line > 0
    for d in range(n):
        slot = line * n + turn(place, n - d)
        if d:
            arrive(cols.at[slot], c1_send.at[d], c1_recv.at[d])
        source = cols.at[slot] if d else blocks.at[place]
        send(source, cols.at[slot], up_send.at[0, d], up_recv.at[0, d], me + n, when=above)
        send(source, cols.at[slot], down_send.at[0, d], down_recv.at[0, d], me - n, when=below)
        slot = turn(line, n - d) * n + place
        if d:
            arrive(rows.at[slot], r1_send.at[d], r1_recv.at[d])
        source = rows.at[slot] if d else blocks.at[line]
        for e in range(1, n):
            send(source, rows.at[slot], r2_send.at[d, e], r2_recv.at[d, e],
                 line * n + turn(place, e))

    for t in range(1, n):
        for d in range(n):
            def from_below(t=t, d=d):
                slot = (line - t) * n + turn(place, n - d)
                arrive(cols.at[slot], up_send.at[t - 1, d], up_recv.at[t - 1, d])

            def from_above(t=t, d=d):
                slot = (line + t) * n + turn(place, n - d)
                arrive(cols.at[slot], down_send.at[t - 1, d], down_recv.at[t - 1, d])

            pl.when(line - t >= 0)(from_below)
            if t < n - 1:
                slot = jnp.maximum(line - t, 0) * n + turn(place, n - d)
                send(cols.at[slot], cols.at[slot], up_send.at[t, d], up_recv.at[t, d], me + n,
                     when=jnp.logical_and(line - t >= 0, above))
            pl.when(line + t < n)(from_above)
            if t < n - 1:
                slot = jnp.minimum(line + t, n - 1) * n + turn(place, n - d)
                send(cols.at[slot], cols.at[slot], down_send.at[t, d], down_recv.at[t, d], me - n,
                     when=jnp.logical_and(line + t < n, below))

    for d in range(n):
        for e in range(1, n):
            slot = turn(line, n - d) * n + turn(place, n - e)
            arrive(rows.at[slot], r2_send.at[d, e], r2_recv.at[d, e])
    own_row.wait()
    own_col.wait()
    for when, wait in pending:
        guarded(when, wait)


def exchange(own, groups, devices, n):
    _, _, states, length = own.shape
    anywhere = pl.BlockSpec(memory_space=pl.ANY)
    side = jax.ShapeDtypeStruct((devices, 2, states, length), jnp.bfloat16)
    sem = pltpu.SemaphoreType.DMA
    rows, cols, _ = pl.pallas_call(
        functools.partial(exchange_kernel, groups, n),
        out_shape=[side, side, jax.ShapeDtypeStruct((n, 2, states, length), jnp.bfloat16)],
        in_specs=[anywhere],
        out_specs=[anywhere] * 3,
        scratch_shapes=[sem((3,)), sem((groups,)), sem((groups,))]
        + [sem((n,))] * 4 + [sem((n, n))] * 6,
        compiler_params=pltpu.CompilerParams(collective_id=0, has_side_effects=True),
        name="exchange",
    )(own)
    return rows, cols


def polar_kernel(partner_ref, row_ref, col_ref, occ_ref, virt_ref, out_ref, right_ref, acc):
    kpoints, parts, bands, row_len = row_ref.shape
    col_len = col_ref.shape[3]
    tile = col_len // 3 if col_len % 384 == 0 else col_len
    scaling = 1.0 / (bands * bands)
    diagonal = lax.broadcasted_iota(jnp.int32, (bands, bands), 0) == lax.broadcasted_iota(
        jnp.int32, (bands, bands), 1
    )

    def left(k, weight_ref):
        weight = jnp.where(diagonal, weight_ref[pl.ds(k, 1), :], 0.0)
        weight = jnp.sum(weight, axis=1, keepdims=True)
        weighted = (row_ref[k].astype(jnp.float32) * weight[None]).astype(jnp.bfloat16)
        real, imag = weighted[0], weighted[1]
        return jnp.concatenate([real, imag], axis=0), jnp.concatenate([imag, -real], axis=0)

    def turn(k, carry):
        cols = col_ref[k]
        right_ref[k] = jnp.concatenate([cols[0], cols[1]], axis=0).T
        return carry

    def step(k, carry):
        other = partner_ref[k]
        occ_left = left(k, occ_ref)
        virt_left = left(other, virt_ref)
        for m in range(col_len // tile):
            rows = slice(m * tile, (m + 1) * tile)
            occ_right, virt_right = right_ref[k, rows], right_ref[other, rows]
            occ_real, occ_imag = [
                jnp.dot(occ_right, value, preferred_element_type=jnp.float32) for value in occ_left
            ]
            virt_real, virt_imag = [
                jnp.dot(virt_right, value, preferred_element_type=jnp.float32) for value in virt_left
            ]
            acc[0, rows] += occ_real * virt_real + occ_imag * virt_imag
            acc[1, rows] += occ_imag * virt_real - occ_real * virt_imag
        return carry

    acc[...] = jnp.zeros_like(acc)
    lax.fori_loop(0, kpoints, turn, 0)
    lax.fori_loop(0, kpoints, step, 0, unroll=4)
    for c in range(parts):
        out_ref[c, 0] = acc[c].T * scaling


def polarizability(partner, row_side, col_side, occ_weight, virt_weight):
    row_len, col_len = row_side.shape[3], col_side.shape[3]
    vmem = pl.BlockSpec(memory_space=pltpu.VMEM)
    return pl.pallas_call(
        polar_kernel,
        out_shape=jax.ShapeDtypeStruct((2, 1, row_len, col_len), jnp.float32),
        in_specs=[pl.BlockSpec(memory_space=pltpu.SMEM), vmem, vmem, vmem, vmem],
        out_specs=vmem,
        scratch_shapes=[
            pltpu.VMEM((col_side.shape[0], col_len, 2 * col_side.shape[2]), jnp.bfloat16),
            pltpu.VMEM((2, col_len, row_len), jnp.float32),
        ],
        compiler_params=pltpu.CompilerParams(vmem_limit_bytes=VMEM_LIMIT),
        name="polarizability",
    )(partner, row_side, col_side, occ_weight, virt_weight)


def body(coefficients, occ_weight, virt_weight, partner, points):
    devices = lax.axis_size("ka")
    groups = lax.axis_size("grp")
    col_blocks = min(16, max(4, devices // 8))
    row_blocks = devices // col_blocks
    kpoints, bands = occ_weight.shape
    point_count = points.shape[0]
    states = coefficients.shape[1]
    row_len = point_count // row_blocks
    col_len = point_count // col_blocks
    own = orbitals_at(coefficients, points, point_count // groups, row_len)
    rows, cols = exchange(own, groups, devices, col_blocks)

    def by_kpoint(side, length):
        side = side.reshape(kpoints, devices // kpoints, 2, states, length)
        return jnp.swapaxes(side, 1, 2).reshape(kpoints, 2, bands, length)

    return polarizability(
        partner, by_kpoint(rows, row_len), by_kpoint(cols, col_len), occ_weight, virt_weight
    )


def solution(mesh):
    return jax.shard_map(
        body,
        mesh=mesh,
        in_specs=(P(None, "ka", None), P(), P(), P("grp"), P()),
        out_specs=P("grp", "ka", None, None),
        check_vma=False,
    )
```
